1024 devices in a mesh: dp: 8 (over z), lat: 64 (over y, x), inner: 2 (over core).
Axes of the slice: x: 8, y: 8, z: 8, core: 2. Of those that a mesh axis runs over, the one named last changes fastest.
Arguments:
- err_main: bfloat16 [1024, 4096], P(('dp', 'lat', 'inner')), may hold values from -6 to 6
- err_aux: bfloat16 [1024, 4096], P(('dp', 'lat', 'inner')), may hold values from -6 to 6
- resid: bfloat16 [1024, 4096], P(('dp', 'lat', 'inner')), may hold values from -6 to 6
- top_idx: int32 [1024, 64], P('dp'), may hold values from 0 to 4194303, as said below
- top_val: bfloat16 [1024, 64], P('dp'), may hold values from 0.099609375 to 3
- aux_idx: int32 [1024, 512], P('dp'), may hold values from 0 to 32767, as said below
- aux_val: bfloat16 [1024, 512], P('dp'), may hold values from 0.099609375 to 3
- blocks: int32 [256], P(('lat', 'inner')), may hold values from -1 to 255, as said below
- dead: int32 [32768], P(('lat', 'inner')), may hold values 0 or 1
- dec_rows: bfloat16 [32768, 4096], P(('lat', 'inner')), may hold values from -0.09375 to 0.09375
Outputs:
- dec_grad: bfloat16 [32768, 4096], P(('lat', 'inner'), 'dp')
- enc_grad: bfloat16 [32768, 4096], P(('lat', 'inner'), 'dp')
The draws below stay inside these ranges and needn't reach their ends.
Inputs may be any that keep to these rules, and one draw needn't show every extreme that they name: `top_idx`: each row holds 64 different latents, all in active blocks. `aux_idx`: each row holds 512 different slots, none in an empty block slot. A shard's first slot is always filled, its filled blocks differ, and some shard fills all 2 slots.
All inputs are finite; a program needn't handle non-finite values. No bound on the sum of `dead` on one device may be relied on, other than what follows from the above.
Results may differ from the reference program's by a relative error of at most 0.018.
Values may be sent and summed in bfloat16 or wider, within the bound.
No kernel may reach another device: no remote copies, remote signals or barrier semaphores. Data moves between devices by JAX's collectives and lax.ppermute only.
A program may use at most 32 MiB of HBM per device.

```python
import math
import jax
import jax.numpy as jnp
from jax import lax

D = 4096
LAT_DEV = 32768
K = 64
KAUX = 512
BLOCK = 128
MAXBLK = 2
TOKENS = 1024
ACTIVE = 32768
N_DP = 8
N_LAT = 64
N_INNER = 2


def pick_blocks(key):
    n_shards = N_LAT * N_INNER
    n_blocks = LAT_DEV // BLOCK
    key_one, key_two, key_three = jax.random.split(jax.random.fold_in(key, 11), 3)
    first = jax.random.randint(key_one, (n_shards,), 0, n_blocks)
    second = (first + 1 + jax.random.randint(key_two, (n_shards,), 0, n_blocks - 1)) % n_blocks
    filled = jax.random.randint(key_three, (n_shards,), 0, 2).at[0].set(1).at[n_shards - 1].set(1)
    second = jnp.where(filled == 1, second, -1)
    return jnp.stack([first, second], axis=1).reshape(-1).astype(jnp.int32)


def pick_slots(key, salt, count):
    table = pick_blocks(key)
    width = MAXBLK * BLOCK
    active = width * N_LAT * N_INNER
    live = jnp.repeat(table >= 0, BLOCK)
    scores = jax.random.randint(jax.random.fold_in(key, salt), (TOKENS, active), 0, 2 ** 14) * active
    scores = scores + jnp.arange(active, dtype=jnp.int32)[None, :]
    scores = jnp.where(live[None, :], scores, -1)
    return lax.top_k(scores, count)[1].astype(jnp.int32)


def draw_top_idx(key, part):
    table = pick_blocks(key)
    width = MAXBLK * BLOCK
    picked = pick_slots(key, 21, K)
    owner = picked // width
    slot = picked // BLOCK % MAXBLK
    block_num = table[owner * MAXBLK + slot]
    return (owner * LAT_DEV + block_num * BLOCK + picked % BLOCK).astype(jnp.int32)


def draw_aux_idx(key, part):
    return pick_slots(key, 22, KAUX)


def draw_blocks(key, part):
    return pick_blocks(key)


def place_ends(values, own_key, least, largest):
    spot = [jax.random.randint(jax.random.fold_in(own_key, axis), (), 0, length) for axis, length in enumerate(values.shape)]
    widest = values.shape.index(max(values.shape))
    neighbour = spot[:widest] + [(spot[widest] + 1) % values.shape[widest]] + spot[widest + 1:]
    return values.at[tuple(spot)].set(least).at[tuple(neighbour)].set(largest)


def steps_of(key, extent, cuts, least, high):
    level, own = 1.0, jax.random.fold_in(key, 6)
    for position, parts in cuts:
        steps = jnp.exp(jax.random.uniform(jax.random.fold_in(own, position), (parts,), jnp.float32, least / len(cuts), high / len(cuts)))
        level = level * jnp.repeat(steps, extent[position] // parts).reshape([-1 if axis == position else 1 for axis in range(len(extent))])
    return level


def bell_draw(stream_key, extent, deviation, limit, shards=(), held_as=jnp.bfloat16):
    drawn = deviation * jax.random.normal(stream_key, extent, jnp.float32)
    if shards:
        drawn = drawn * steps_of(stream_key, extent, shards, -0.22, 0.18)
    return jnp.clip(drawn, -limit, limit).astype(held_as)


def setup_inputs(seed: int = 0) -> dict:
    seeds = jax.random.split(jax.random.key(seed), 11)
    err_main = bell_draw(seeds[0], (TOKENS, D), 1.0, 6.0, ((0, 1024),))
    err_aux = bell_draw(seeds[1], (TOKENS, D), 1.0, 6.0, ((0, 1024),))
    resid = bell_draw(seeds[2], (TOKENS, D), 1.0, 6.0, ((0, 1024),))
    top_idx = draw_top_idx(jax.random.fold_in(seeds[10], 71), 0)
    top_val = jnp.clip(jnp.exp(math.log(3.0) - 3.4051113 * jax.random.uniform(seeds[4], (TOKENS, K), jnp.float32) ** steps_of(seeds[4], (TOKENS, K), ((0, 8),), -0.2, 0.2)), 0.099609375, 3.0).astype(jnp.bfloat16)
    aux_idx = draw_aux_idx(jax.random.fold_in(seeds[10], 71), 0)
    aux_val = jnp.clip(jnp.exp(math.log(3.0) - 3.4051113 * jax.random.uniform(seeds[6], (TOKENS, KAUX), jnp.float32) ** steps_of(seeds[6], (TOKENS, KAUX), ((0, 8),), -0.2, 0.2)), 0.099609375, 3.0).astype(jnp.bfloat16)
    blocks = draw_blocks(jax.random.fold_in(seeds[10], 71), 0)
    dead = place_ends((jax.random.randint(seeds[8], (ACTIVE,), 0, 2) < 1).astype(jnp.int32), jax.random.fold_in(seeds[8], 1), 0, 1)
    dec_rows = bell_draw(seeds[9], (ACTIVE, D), D ** -0.5, 0.09375, ((0, 128),))
    return {"err_main": err_main, "err_aux": err_aux, "resid": resid, "top_idx": top_idx, "top_val": top_val, "aux_idx": aux_idx, "aux_val": aux_val, "blocks": blocks, "dead": dead, "dec_rows": dec_rows}


def reference(err_main, err_aux, resid, top_idx, top_val, aux_idx, aux_val, blocks, dead, dec_rows):
    n_shards = N_LAT * N_INNER
    width = MAXBLK * BLOCK
    total = err_main.shape[0]
    group = total // N_DP
    table = blocks.reshape(n_shards, MAXBLK)
    slot_ids = jnp.arange(MAXBLK, dtype=jnp.int32)

    def place(ids):
        owner = ids // LAT_DEV
        local = ids % LAT_DEV
        row = table[owner]
        slot = jnp.sum(jnp.where(row == (local // BLOCK)[..., None], slot_ids, 0), axis=-1)
        return owner, (slot * BLOCK + local % BLOCK).astype(jnp.int32)

    main_owner, main_col = place(top_idx)
    aux_owner = (aux_idx // width).astype(jnp.int32)
    aux_col = (aux_idx % width).astype(jnp.int32)
    tok_ids = jnp.arange(total, dtype=jnp.int32)[:, None]
    main_f = err_main.astype(jnp.float32).reshape(N_DP, group, -1)
    aux_f = err_aux.astype(jnp.float32).reshape(N_DP, group, -1)
    resid_f = resid.astype(jnp.float32).reshape(N_DP, group, -1)

    def select(owner, col, vals, shard):
        cols = jnp.where(owner == shard, col, width).astype(jnp.int32)
        table_out = jnp.zeros((total, width + 1), jnp.float32).at[tok_ids, cols].add(vals.astype(jnp.float32))
        return table_out[:, :width]

    def per_shard(shard):
        dec = lax.dynamic_slice_in_dim(dec_rows, (shard * width).astype(jnp.int32), width, 0)
        dead_f = lax.dynamic_slice_in_dim(dead, (shard * width).astype(jnp.int32), width, 0).astype(jnp.float32)
        sel_main = select(main_owner, main_col, top_val, shard)
        sel_aux = select(aux_owner, aux_col, aux_val, shard) * dead_f[None, :]
        dval_main = jnp.dot(err_main, dec.T, preferred_element_type=jnp.float32)
        dval_aux = jnp.dot(err_aux, dec.T, preferred_element_type=jnp.float32)
        dpre = (jnp.where(sel_main > 0, dval_main, 0.0) + jnp.where(sel_aux > 0, dval_aux, 0.0)).astype(jnp.bfloat16)
        sm = sel_main.reshape(N_DP, group, width)
        sa = sel_aux.reshape(N_DP, group, width)
        dp_f = dpre.astype(jnp.float32).reshape(N_DP, group, width)
        part_dec = jnp.einsum("gtl,gtd->gld", sm, main_f) + jnp.einsum("gtl,gtd->gld", sa, aux_f)
        part_enc = jnp.einsum("gtl,gtd->gld", dp_f, resid_f)
        part_dec = part_dec.astype(jnp.bfloat16).astype(jnp.float32)
        part_enc = part_enc.astype(jnp.bfloat16).astype(jnp.float32)
        return jnp.sum(part_dec, axis=0).astype(jnp.bfloat16), jnp.sum(part_enc, axis=0).astype(jnp.bfloat16)

    dec_all, enc_all = lax.map(per_shard, jnp.arange(n_shards, dtype=jnp.int32))
    return dec_all.reshape(n_shards * width, -1), enc_all.reshape(n_shards * width, -1)
```

```python
import jax
import jax.numpy as jnp
from jax import lax
from jax.experimental import pallas as pl
from jax.experimental.pallas import tpu as pltpu
from jax.sharding import PartitionSpec as P

LAT_DEV = 32768
BLOCK = 128


def sel_kernel(n_main, n_aux, main_col, main_val, aux_col, aux_val, dead, out):
    slots = dead.shape[1]
    lanes = [lax.broadcasted_iota(jnp.int32, (8, 128), 1) + 128 * k for k in range(slots // 128)]

    def place(acc, col, val, width):
        for j in range(width):
            c = jnp.broadcast_to(col[:, j : j + 1], (8, 128))
            v = jnp.broadcast_to(val[:, j : j + 1], (8, 128))
            acc = [jnp.where(c == lane, v, a) for lane, a in zip(lanes, acc)]
        return acc

    zero = [jnp.zeros((8, 128), jnp.float32) for _ in lanes]
    main = place(zero, main_col[...], main_val[...], n_main)

    def step(i, acc):
        part = pl.ds(pl.multiple_of(i * 128, 128), 128)
        return tuple(place(list(acc), aux_col[:, part], aux_val[:, part], 128))

    aux = lax.fori_loop(0, n_aux // 128, step, tuple(zero))
    for k in range(len(lanes)):
        out[:, 128 * k : 128 * k + 128] = main[k]
        out[:, slots + 128 * k : slots + 128 * k + 128] = (
            aux[k] * dead[:, 128 * k : 128 * k + 128]
        )


def make_sel(main_col, main_val, aux_col, aux_val, dead):
    rows, n_main = main_col.shape
    n_aux = aux_col.shape[1]
    slots = dead.shape[1]

    def spec(width):
        return pl.BlockSpec((8, width), lambda i: (i, 0))

    def kernel(*refs):
        sel_kernel(n_main, n_aux, *refs)

    return pl.pallas_call(
        kernel,
        grid=(rows // 8,),
        in_specs=[spec(n_main), spec(n_main), spec(n_aux), spec(n_aux)]
        + [pl.BlockSpec((1, slots), lambda i: (0, 0))],
        out_specs=spec(2 * slots),
        out_shape=jax.ShapeDtypeStruct((rows, 2 * slots), jnp.float32),
        cost_estimate=pl.CostEstimate(
            flops=rows * n_aux * slots * 8, bytes_accessed=1 << 20, transcendentals=0
        ),
        name="sel",
    )(main_col, main_val, aux_col, aux_val, dead)


def rows_dot(left, right):
    return lax.dot_general(
        left, right, (((1,), (1,)), ((), ())), preferred_element_type=jnp.float32
    )


def cols_dot(left, right):
    return lax.dot_general(
        left, right, (((0,), (0,)), ((), ())), preferred_element_type=jnp.float32
    )


def local(
    n_dp, n_lat, n_in, err_main, err_aux, resid, top_idx, top_val, aux_idx, aux_val, blocks, dead, dec_rows
):
    width, d = dec_rows.shape
    cols = d // n_dp
    group = top_idx.shape[0]
    mine = group // n_in
    slots = width * n_in
    dp = lax.axis_index("dp")
    lat = lax.axis_index("lat")
    core = lax.axis_index("inner")

    rows = jnp.concatenate([err_main, err_aux, resid, resid], axis=0)
    rows = rows.reshape(4, n_dp, cols).transpose(1, 0, 2)
    rows = lax.all_to_all(rows, "dp", 0, 0, tiled=True)
    rows = rows[:, :3].transpose(1, 0, 2).reshape(3 * n_dp, cols)
    rows = lax.all_to_all(
        jnp.broadcast_to(rows[None], (n_lat,) + rows.shape), "lat", 0, 0, tiled=True
    )
    rows = rows.reshape(n_lat, 3, n_dp, cols).transpose(1, 2, 0, 3).reshape(3, n_dp * n_lat, cols)
    main, aux, res = rows[0], rows[1], rows[2]

    dec = lax.all_gather(
        lax.dynamic_slice_in_dim(dec_rows, dp * cols, cols, 1), "inner", axis=0, tiled=True
    )
    table = lax.all_gather(blocks, "inner", axis=0, tiled=True)
    dead_all = lax.all_gather(dead, "inner", axis=0, tiled=True)

    def own(v):
        return lax.dynamic_index_in_dim(v.reshape(mine, n_in, -1), core, 1, keepdims=False)

    top_own, aux_own = own(top_idx), own(aux_idx)
    per = table.shape[0] // n_in
    keys = jnp.where(
        table >= 0,
        (lat * n_in + jnp.arange(table.shape[0], dtype=jnp.int32) // per) * (LAT_DEV // BLOCK) + table,
        -1,
    )
    main_col = jnp.full(top_own.shape, -1, jnp.int32)
    for k in range(table.shape[0]):
        main_col = jnp.where(top_own // BLOCK == keys[k], k * BLOCK + top_own % BLOCK, main_col)
    sel = make_sel(
        main_col,
        own(top_val).astype(jnp.float32),
        aux_own - lat * slots,
        own(aux_val).astype(jnp.float32),
        dead_all.astype(jnp.float32)[None],
    ).astype(jnp.bfloat16)
    sel = lax.all_gather(sel, "dp", axis=0, tiled=True)
    sel_main, sel_aux = sel[:, :slots], sel[:, slots:]

    part = (
        jnp.where(sel_main > 0, rows_dot(main, dec), 0.0)
        + jnp.where(sel_aux > 0, rows_dot(aux, dec), 0.0)
    ).astype(jnp.bfloat16)
    part = lax.all_to_all(part.reshape(n_dp, n_lat, slots), "dp", 0, 0, tiled=True)
    dpre = jnp.sum(part.astype(jnp.float32), axis=0).astype(jnp.bfloat16)
    dpre = lax.all_to_all(
        jnp.broadcast_to(dpre[None], (n_dp,) + dpre.shape), "dp", 0, 0, tiled=True
    ).reshape(n_dp * n_lat, slots)

    swap = [(i, (i + 1) % n_in) for i in range(n_in)]

    def over_cores(term):
        theirs = lax.dynamic_slice_in_dim(term, (1 - core) * width, width, 0).astype(jnp.bfloat16)
        ours = lax.dynamic_slice_in_dim(term, core * width, width, 0)
        got = lax.ppermute(theirs, "inner", swap)
        return (ours + got.astype(jnp.float32)).astype(jnp.bfloat16)

    dec_grad = over_cores(cols_dot(sel_main, main) + cols_dot(sel_aux, aux))
    enc_grad = over_cores(cols_dot(dpre, res))
    return (dec_grad, enc_grad)


def solution(mesh):
    tokens = P(("dp", "lat", "inner"), None)
    shard = ("lat", "inner")
    in_specs = (tokens,) * 3 + (P("dp", None),) * 4 + (P(shard), P(shard), P(shard, None))
    out_specs = (P(shard, "dp"), P(shard, "dp"))
    n_dp, n_lat, n_in = (mesh.shape[a] for a in ("dp", "lat", "inner"))

    def step(*args):
        return local(n_dp, n_lat, n_in, *args)

    return jax.shard_map(step, mesh=mesh, in_specs=in_specs, out_specs=out_specs, check_vma=False)
```

```python
import math

import jax
import jax.numpy as jnp
from jax import lax
from jax.experimental import pallas as pl
from jax.experimental.pallas import tpu as pltpu
from jax.sharding import PartitionSpec as P

LAT_DEV = 32768
BLOCK = 128
STEPS = 2048
BITS = 13


def sel_kernel(place_ref, top_idx, top_val, aux_idx, aux_val, dead, out, packed, found):
    slots = dead.shape[1]
    n_aux = aux_idx.shape[1]
    n_top = top_idx.shape[1]
    rows = top_idx.shape[0]
    side = math.isqrt(rows // 2)
    core, lat = place_ref[0], place_ref[1]
    n_blocks = slots // BLOCK

    def pack(col, val):
        return col * (1 << BITS) + (val[...].astype(jnp.float32) * STEPS).astype(jnp.int32)

    col = aux_idx[...] - lat * slots
    col = jnp.where((col >= 0) & (col < slots), (col + core * (slots // 2)) & (slots - 1), -1)
    col = pack(col, aux_val)
    for i in range(n_aux // 128):
        packed[rows * i : rows * (i + 1), :] = col[:, 128 * i : 128 * (i + 1)]
    block, inside = top_idx[...] >> 7, top_idx[...] & (BLOCK - 1)
    col = jnp.full(top_idx.shape, -1, jnp.int32)
    for m in range(n_blocks):
        col = jnp.where(block == place_ref[2 + m], m * BLOCK + inside, col)
    packed[rows * (n_aux // 128) :, :n_top] = pack(col, top_val)

    lanes = [lax.broadcasted_iota(jnp.int32, (side, 128), 1) + 128 * k for k in range(slots // 128)]
    zero = tuple(jnp.zeros((side, 128), jnp.int32) for _ in lanes)

    def step(a, carry):
        def put(acc, i, width):
            along_x = packed[pl.ds(rows * i + 2 * side * a, side, stride=2), :]
            along_y = packed[pl.ds(rows * i + 2 * a + 1, side, stride=2 * side), :]
            part = jnp.where(core == 0, along_x, along_y)
            for j in range(width):
                v = jnp.broadcast_to(part[:, j : j + 1], (side, 128))
                c = v >> BITS
                acc = [jnp.where(c == lane, v, a) for lane, a in zip(lanes, acc)]
            return tuple(acc)

        main = put(zero, n_aux // 128, n_top)
        aux = lax.fori_loop(0, n_aux // 128, lambda i, acc: put(acc, i, 128), zero)
        to = pl.ds(pl.multiple_of(a * side, side), side)
        for k in range(len(lanes)):
            found[to, 128 * k : 128 * k + 128] = main[k]
            found[to, slots + 128 * k : slots + 128 * k + 128] = aux[k]
        return carry

    lax.fori_loop(0, side, step, 0)
    value = (found[...] & ((1 << BITS) - 1)).astype(jnp.float32) * (1.0 / STEPS)
    out[:, :slots] = value[:, :slots].astype(jnp.bfloat16)
    out[:, slots:] = (value[:, slots:] * dead[...].astype(jnp.float32)).astype(jnp.bfloat16)


def make_sel(place, top_idx, top_val, aux_idx, aux_val, dead):
    rows = top_idx.shape[0]
    parts = aux_idx.shape[1] // 128 + 1
    slots = dead.shape[1]
    whole = pl.BlockSpec(memory_space=pltpu.VMEM)
    return pl.pallas_call(
        sel_kernel,
        in_specs=[pl.BlockSpec(memory_space=pltpu.SMEM)] + [whole] * 5,
        out_specs=whole,
        out_shape=jax.ShapeDtypeStruct((rows // 2, 2 * slots), jnp.bfloat16),
        scratch_shapes=[
            pltpu.VMEM((rows * parts, 128), jnp.int32),
            pltpu.VMEM((rows // 2, 2 * slots), jnp.int32),
        ],
        cost_estimate=pl.CostEstimate(
            flops=rows * parts * 128 * slots * 32, bytes_accessed=1 << 20, transcendentals=0
        ),
        name="sel",
    )(place, top_idx, top_val, aux_idx, aux_val, dead)


def rows_dot(left, right):
    return lax.dot_general(
        left, right, (((1,), (1,)), ((), ())), preferred_element_type=jnp.float32
    )


def cols_dot(left, right):
    return lax.dot_general(
        left, right, (((0,), (0,)), ((), ())), preferred_element_type=jnp.float32
    )


def plane_groups(n_dp, side, n_in):
    def device(z, y, x, c):
        return ((z * side + y) * side + x) * n_in + c

    ranks = range(side)
    along_x = [[[device(z, y, x, c) for x in ranks] for z in range(n_dp) for y in ranks] for c in range(2)]
    along_y = [[[device(z, y, x, c) for y in ranks] for z in range(n_dp) for x in ranks] for c in range(2)]
    return along_x[0] + along_y[1], along_y[0] + along_x[1]


def local(
    n_dp, n_lat, n_in, err_main, err_aux, resid, top_idx, top_val, aux_idx, aux_val, blocks, dead, dec_rows
):
    width, d = dec_rows.shape
    cols = d // n_dp
    slots = width * n_in
    side = math.isqrt(n_lat)
    dp = lax.axis_index("dp")
    lat = lax.axis_index("lat")
    core = lax.axis_index("inner")
    swap = [(i, (i + 1) % n_in) for i in range(n_in)]
    first, second = plane_groups(n_dp, side, n_in)

    def grow(v, step):
        got = lax.ppermute(v, "dp", [(i, i ^ step) for i in range(n_dp)])
        return jnp.concatenate([v, got], axis=0)

    def spread(v, groups):
        return lax.all_to_all(
            jnp.broadcast_to(v[None], (side,) + v.shape),
            ("dp", "lat", "inner"), 0, 0, axis_index_groups=groups, tiled=True,
        )

    full = jnp.concatenate([err_main, err_aux], axis=0)
    cut = jnp.concatenate([full, resid, resid], axis=0).reshape(4, n_dp, cols).transpose(1, 0, 2)
    cut = lax.all_to_all(cut, "dp", 0, 0, tiled=True)
    cut = cut[:, :3].reshape(2, 2, 2, 3, cols)
    for bit in range(3):
        cut = jnp.where((dp >> bit) & 1 == 1, jnp.flip(cut, 2 - bit), cut)
    cut = cut.transpose(3, 2, 1, 0, 4).reshape(2, 3 * n_dp * cols // 2)

    near = spread(jnp.concatenate([full, cut], axis=1), first)
    full = spread(near[:, :, :d], second)
    part = spread(near[:, :, d:].reshape(side, 3 * n_dp, cols), second)
    part = part.reshape(n_lat, 3, n_dp, cols)
    main, aux, res = (part[:, i].reshape(n_lat * n_dp, cols) for i in range(3))

    dec_other = lax.ppermute(dec_rows, "inner", swap)
    small = jnp.concatenate([dead, blocks, jnp.zeros((128 - blocks.shape[0],), jnp.int32)])
    small_other = lax.ppermute(small, "inner", swap)
    dead_all = jnp.concatenate([dead, small_other[:width]])[None]
    table = jnp.concatenate([blocks, small_other[width : width + blocks.shape[0]]])
    owner = lat * n_in + (core + jnp.arange(table.shape[0], dtype=jnp.int32) // blocks.shape[0]) % n_in
    keys = jnp.where(table >= 0, owner * (LAT_DEV // BLOCK) + table, -1)
    place = jnp.concatenate([jnp.stack([core, lat]), keys])
    sel = make_sel(place, top_idx, top_val, aux_idx, aux_val, dead_all)
    sel_all = grow(sel[None], 4)
    sel_all, full = lax.optimization_barrier((sel_all, full))
    sel_all = grow(grow(sel_all, 2), 1).transpose(1, 0, 2).reshape(n_lat * n_dp, 2 * slots)

    both = full.reshape(n_lat, 2, d).transpose(1, 0, 2).reshape(2 * n_lat, d)
    dval = jnp.concatenate([rows_dot(both, dec_rows), rows_dot(both, dec_other)], axis=1)
    dpre = jnp.where(sel[:, :slots] > 0, dval[:n_lat], 0.0) + jnp.where(
        sel[:, slots:] > 0, dval[n_lat:], 0.0
    )
    dpre_all = grow(grow(grow(dpre.astype(jnp.bfloat16)[None], 4), 2), 1)
    dpre_all = dpre_all.transpose(1, 0, 2).reshape(n_lat * n_dp, slots)

    def half(other):
        def pick(table, i):
            return table[:, i * slots + other * width : i * slots + (other + 1) * width]

        dec_term = cols_dot(pick(sel_all, 0), main) + cols_dot(pick(sel_all, 1), aux)
        return dec_term, cols_dot(pick(dpre_all, 0), res)

    sent = jnp.stack(half(1)).astype(jnp.bfloat16)
    got = lax.ppermute(sent, "inner", swap).astype(jnp.float32)
    dec_term, enc_term = half(0)
    return ((dec_term + got[0]).astype(jnp.bfloat16), (enc_term + got[1]).astype(jnp.bfloat16))


def solution(mesh):
    tokens = P(("dp", "lat", "inner"), None)
    shard = ("lat", "inner")
    in_specs = (tokens,) * 3 + (P("dp", None),) * 4 + (P(shard), P(shard), P(shard, None))
    out_specs = (P(shard, "dp"), P(shard, "dp"))
    n_dp, n_lat, n_in = (mesh.shape[a] for a in ("dp", "lat", "inner"))

    def step(*args):
        return local(n_dp, n_lat, n_in, *args)

    return jax.shard_map(step, mesh=mesh, in_specs=in_specs, out_specs=out_specs, check_vma=False)
```

```python
import math

import jax
import jax.numpy as jnp
from jax import lax
from jax.experimental import pallas as pl
from jax.experimental.pallas import tpu as pltpu
from jax.sharding import PartitionSpec as P

LAT_DEV = 32768
BLOCK = 128


def sel_kernel(place, top_idx, top_val, aux_idx, aux_val, dead, out, high, low, val, found):
    rows, n_top = top_idx.shape
    n_aux = aux_idx.shape[1]
    slots = dead.shape[1]
    side = math.isqrt(rows // 2)
    tables = 2 * slots // 128
    core = place[0]

    def put(at, col, v):
        to = pl.ds(at, col.shape[1])
        high[:, to] = col >> 7
        low[:, to] = col & 127
        val[:, to] = v[...].astype(jnp.float32)

    col = aux_idx[...] - place[1] * slots
    inside = (col >= 0) & (col < slots)
    put(0, jnp.where(inside, slots + ((col + core * (slots // 2)) & (slots - 1)), -1), aux_val)
    block, inside = top_idx[...] >> 7, top_idx[...] & (BLOCK - 1)
    col = jnp.full(top_idx.shape, -1, jnp.int32)
    for m in range(slots // BLOCK):
        col = jnp.where(block == place[2 + m], m * BLOCK + inside, col)
    put(n_aux, col, top_val)

    n = n_aux + n_top
    row_high = lax.broadcasted_iota(jnp.int32, (tables, n), 0)
    row_low = lax.broadcasted_iota(jnp.int32, (128, n), 0)

    def step(a, carry):
        for b in range(side):
            row = jnp.where(core == 0, 2 * (side * a + b), 2 * (side * b + a) + 1)
            one = pl.ds(row, 1)
            spread = jnp.where(row_high == high[one, :n], val[one, :n], 0.0).astype(jnp.bfloat16)
            hot = jnp.where(row_low == low[one, :n], 1.0, 0.0).astype(jnp.bfloat16)
            table = lax.dot_general(
                spread, hot, (((1,), (1,)), ((), ())), preferred_element_type=jnp.float32
            )
            found[pl.ds(side * a + b, tables, stride=side * side), :] = table
        return carry

    lax.fori_loop(0, side, step, 0)
    for k in range(tables):
        table = found[side * side * k : side * side * (k + 1), :]
        if 128 * k >= slots:
            table = table * dead[:, 128 * k - slots : 128 * (k + 1) - slots].astype(jnp.float32)
        out[:, 128 * k : 128 * (k + 1)] = table.astype(out.dtype)


def make_sel(place, top_idx, top_val, aux_idx, aux_val, dead):
    rows, n_top = top_idx.shape
    entries = aux_idx.shape[1] + 128
    slots = dead.shape[1]
    whole = pl.BlockSpec(memory_space=pltpu.VMEM)
    return pl.pallas_call(
        sel_kernel,
        in_specs=[pl.BlockSpec(memory_space=pltpu.SMEM)] + [whole] * 5,
        out_specs=whole,
        out_shape=jax.ShapeDtypeStruct((rows // 2, 2 * slots), jnp.bfloat16),
        scratch_shapes=[
            pltpu.VMEM((rows, entries), jnp.int32),
            pltpu.VMEM((rows, entries), jnp.int32),
            pltpu.VMEM((rows, entries), jnp.float32),
            pltpu.VMEM((rows * slots // 128, 128), jnp.float32),
        ],
        cost_estimate=pl.CostEstimate(
            flops=rows * entries * slots * 32, bytes_accessed=1 << 20, transcendentals=0
        ),
        name="sel",
    )(place, top_idx, top_val, aux_idx, aux_val, dead)


def rows_dot(left, right):
    return lax.dot_general(
        left, right, (((1,), (1,)), ((), ())), preferred_element_type=jnp.float32
    )


def cols_dot(left, right):
    return lax.dot_general(
        left, right, (((0,), (0,)), ((), ())), preferred_element_type=jnp.float32
    )


def plane_groups(n_dp, side, n_in):
    def device(z, a, b, c):
        y, x = (a, b) if c == 0 else (b, a)
        return ((z * side + y) * side + x) * n_in + c

    ranks, dps, cores = range(side), range(n_dp), range(n_in)
    first = [[device(z, a, b, c) for b in ranks] for z in dps for a in ranks for c in cores]
    wide = [[device(z, a, b, c) for z in dps for b in ranks] for a in ranks for c in cores]
    second = [[device(z, a, b, c) for a in ranks] for z in dps for b in ranks for c in cores]
    return first, wide, second


def local(
    n_dp, n_lat, n_in, err_main, err_aux, resid, top_idx, top_val, aux_idx, aux_val, blocks, dead, dec_rows
):
    width, d = dec_rows.shape
    cols = d // n_dp
    slots = width * n_in
    side = math.isqrt(n_lat)
    dp = lax.axis_index("dp")
    lat = lax.axis_index("lat")
    core = lax.axis_index("inner")
    swap = [(i, (i + 1) % n_in) for i in range(n_in)]
    first, wide, second = plane_groups(n_dp, side, n_in)

    def send(v, step):
        return lax.ppermute(v, "dp", [(i, i ^ step) for i in range(n_dp)])

    def grow(v, step):
        return jnp.concatenate([v, send(v, step)], axis=0)

    def exchange(v, groups):
        return lax.all_to_all(v, ("dp", "lat", "inner"), 0, 0, axis_index_groups=groups, tiled=True)

    def spread(v, groups):
        return exchange(jnp.broadcast_to(v[None], (side,) + v.shape), groups)

    dec_other = lax.ppermute(dec_rows, "inner", swap)
    small = jnp.concatenate([dead, blocks, jnp.zeros((128 - blocks.shape[0],), jnp.int32)])
    small_other = lax.ppermute(small, "inner", swap)
    dead_all = jnp.concatenate([dead, small_other[:width]])[None]
    table = jnp.concatenate([blocks, small_other[width : width + blocks.shape[0]]])
    owner = lat * n_in + (core + jnp.arange(table.shape[0], dtype=jnp.int32) // blocks.shape[0]) % n_in
    keys = jnp.where(table >= 0, owner * (LAT_DEV // BLOCK) + table, -1)
    place = jnp.concatenate([jnp.stack([core, lat]), keys])
    sel = make_sel(place, top_idx, top_val, aux_idx, aux_val, dead_all)

    near = spread(jnp.concatenate([err_main, err_aux], axis=0), first)
    near, sel = lax.optimization_barrier((near, sel))
    full = spread(near, second)
    sel_all = grow(sel[None], 4)

    both = full.reshape(n_lat, 2, d).transpose(1, 0, 2).reshape(2 * n_lat, d)
    dval = jnp.concatenate([rows_dot(both, dec_rows), rows_dot(both, dec_other)], axis=1)
    dpre = jnp.where(sel[:, :slots] > 0, dval[:n_lat], 0.0) + jnp.where(
        sel[:, slots:] > 0, dval[n_lat:], 0.0
    )

    cut = jnp.concatenate([err_main, err_aux, resid, resid], axis=0)
    cut = cut.reshape(4, n_dp, cols).transpose(1, 0, 2)
    cut, sel_all = lax.optimization_barrier((cut, sel_all))
    cut = jnp.broadcast_to(cut[:, None], (n_dp, side, 4, cols)).reshape(n_dp * side, 4, cols)
    cut = exchange(cut, wide).reshape(2, 2, 2, side, 4, cols)
    sel_all = grow(sel_all, 2)
    dpre_all = grow(dpre.astype(jnp.bfloat16)[None], 4)
    cut, sel_all, dpre_all = lax.optimization_barrier((cut, sel_all, dpre_all))
    for bit in range(3):
        cut = jnp.where((dp >> bit) & 1 == 1, jnp.flip(cut, 2 - bit), cut)
    cut = cut[..., :3, :].transpose(3, 4, 2, 1, 0, 5).reshape(side, 3 * n_dp, cols)
    part = spread(cut, second).reshape(n_lat, 3, n_dp, cols)
    main, aux, res = (part[:, i].reshape(n_lat * n_dp, cols) for i in range(3))
    sel_all = grow(sel_all, 1).transpose(1, 0, 2).reshape(n_lat * n_dp, 2 * slots)
    dpre_all = jnp.concatenate([dpre_all] + [send(dpre_all, step) for step in (2, 1, 3)], axis=0)
    dpre_all = dpre_all.transpose(1, 0, 2).reshape(n_lat * n_dp, slots)

    def half(other):
        def pick(table, i):
            return table[:, i * slots + other * width : i * slots + (other + 1) * width]

        dec_term = cols_dot(pick(sel_all, 0), main) + cols_dot(pick(sel_all, 1), aux)
        return dec_term, cols_dot(pick(dpre_all, 0), res)

    sent = jnp.stack(half(1)).astype(jnp.bfloat16)
    got = lax.ppermute(sent, "inner", swap).astype(jnp.float32)
    dec_term, enc_term = half(0)
    return ((dec_term + got[0]).astype(jnp.bfloat16), (enc_term + got[1]).astype(jnp.bfloat16))


def solution(mesh):
    tokens = P(("dp", "lat", "inner"), None)
    shard = ("lat", "inner")
    in_specs = (tokens,) * 3 + (P("dp", None),) * 4 + (P(shard), P(shard), P(shard, None))
    out_specs = (P(shard, "dp"), P(shard, "dp"))
    n_dp, n_lat, n_in = (mesh.shape[a] for a in ("dp", "lat", "inner"))

    def step(*args):
        return local(n_dp, n_lat, n_in, *args)

    return jax.shard_map(step, mesh=mesh, in_specs=in_specs, out_specs=out_specs, check_vma=False)
```

```python
import math

import jax
import jax.numpy as jnp
from jax import lax
from jax.experimental import pallas as pl
from jax.experimental.pallas import tpu as pltpu
from jax.sharding import PartitionSpec as P

LAT_DEV = 32768
BLOCK = 128


def sel_kernel(place, top_idx, top_val, aux_idx, aux_val, cores, out, high, low, val, found):
    n_top, rows = top_idx.shape
    n_aux = aux_idx.shape[1]
    slots = out.shape[1] // 2
    width = slots // 2
    side = math.isqrt(rows // 2)
    tables = 2 * slots // 128
    core = place[0]

    def put(at, col, v):
        to = pl.ds(at, col.shape[1])
        high[:, to] = col >> 7
        low[:, to] = col & 127
        val[:, to] = v

    col = aux_idx[...] - place[1] * slots
    inside = (col >= 0) & (col < slots)
    put(0, jnp.where(inside, slots + ((col + core * width) & (slots - 1)), -1), aux_val[...].astype(jnp.float32))
    block, inside = top_idx[...] >> 7, top_idx[...] & (BLOCK - 1)
    col = jnp.full(top_idx.shape, -1, jnp.int32)
    for m in range(slots // BLOCK):
        other, at = divmod(m, width // BLOCK)
        shard = 2 * place[1] + (core if other == 0 else 1 - core)
        number = cores[other : other + 1, width + at : width + at + 1]
        here = (block == number + shard * (LAT_DEV // BLOCK)) & (number >= 0)
        col = jnp.where(here, m * BLOCK + inside, col)
    put(n_aux, col.T, top_val[...].astype(jnp.float32).T)

    n = n_aux + n_top
    row_high = lax.broadcasted_iota(jnp.int32, (tables, n), 0)
    row_low = lax.broadcasted_iota(jnp.int32, (128, n), 0)

    def step(a, carry):
        for b in range(side):
            row = jnp.where(core == 0, 2 * (side * a + b), 2 * (side * b + a) + 1)
            one = pl.ds(row, 1)
            spread = jnp.where(row_high == high[one, :n], val[one, :n], 0.0).astype(jnp.bfloat16)
            hot = jnp.where(row_low == low[one, :n], 1.0, 0.0).astype(jnp.bfloat16)
            table = lax.dot_general(
                spread, hot, (((1,), (1,)), ((), ())), preferred_element_type=jnp.float32
            )
            found[pl.ds(side * a + b, tables, stride=side * side), :] = table
        return carry

    lax.fori_loop(0, side, step, 0)
    for k in range(tables):
        table = found[side * side * k : side * side * (k + 1), :]
        if 128 * k >= slots:
            other, at = divmod(128 * k - slots, width)
            table = table * cores[other : other + 1, at : at + 128].astype(jnp.float32)
        out[:, 128 * k : 128 * (k + 1)] = table.astype(out.dtype)


def make_sel(place, top_idx, top_val, aux_idx, aux_val, cores, slots):
    rows = aux_idx.shape[0]
    entries = aux_idx.shape[1] + 128
    whole = pl.BlockSpec(memory_space=pltpu.VMEM)
    return pl.pallas_call(
        sel_kernel,
        in_specs=[pl.BlockSpec(memory_space=pltpu.SMEM)] + [whole] * 5,
        out_specs=whole,
        out_shape=jax.ShapeDtypeStruct((rows // 2, 2 * slots), jnp.bfloat16),
        scratch_shapes=[
            pltpu.VMEM((rows, entries), jnp.int32),
            pltpu.VMEM((rows, entries), jnp.int32),
            pltpu.VMEM((rows, entries), jnp.float32),
            pltpu.VMEM((rows * slots // 128, 128), jnp.float32),
        ],
        cost_estimate=pl.CostEstimate(
            flops=rows * entries * slots * 32, bytes_accessed=1 << 20, transcendentals=0
        ),
        name="sel",
    )(place, top_idx.T, top_val.T, aux_idx, aux_val, cores)


def rows_dot(left, right):
    return lax.dot_general(
        left, right, (((1,), (1,)), ((), ())), preferred_element_type=jnp.float32
    )


def cols_dot(left, right):
    return lax.dot_general(
        left, right, (((0,), (0,)), ((), ())), preferred_element_type=jnp.float32
    )


def plane_groups(n_dp, side, n_in):
    def device(z, a, b, c):
        y, x = (a, b) if c == 0 else (b, a)
        return ((z * side + y) * side + x) * n_in + c

    ranks, dps, cores = range(side), range(n_dp), range(n_in)
    plane = [[device(z, a, b, c) for a in ranks for b in ranks] for z in dps for c in cores]
    wide = [[device(z, a, b, c) for z in dps for b in ranks] for a in ranks for c in cores]
    second = [[device(z, a, b, c) for a in ranks] for z in dps for b in ranks for c in cores]
    return plane, wide, second


def local(
    n_dp, n_lat, n_in, err_main, err_aux, resid, top_idx, top_val, aux_idx, aux_val, blocks, dead, dec_rows
):
    width, d = dec_rows.shape
    cols = d // n_dp
    slots = width * n_in
    side = math.isqrt(n_lat)
    dp = lax.axis_index("dp")
    lat = lax.axis_index("lat")
    core = lax.axis_index("inner")
    swap = [(i, (i + 1) % n_in) for i in range(n_in)]
    plane, wide, second = plane_groups(n_dp, side, n_in)

    def send(v, step):
        return lax.ppermute(v, "dp", [(i, i ^ step) for i in range(n_dp)])

    def grow(v, step):
        return jnp.concatenate([v, send(v, step)], axis=0)

    def exchange(v, groups):
        return lax.all_to_all(v, ("dp", "lat", "inner"), 0, 0, axis_index_groups=groups, tiled=True)

    def spread(v, groups):
        return exchange(jnp.broadcast_to(v[None], (side,) + v.shape), groups)

    dec_other = lax.ppermute(dec_rows, "inner", swap)
    small = jnp.concatenate([dead, blocks, jnp.zeros((128 - blocks.shape[0],), jnp.int32)])
    small_other = lax.ppermute(small, "inner", swap)
    cores = jnp.stack([small, small_other])
    place = jnp.stack([core, lat])
    sel = make_sel(place, top_idx, top_val, aux_idx, aux_val, cores, slots)

    full = jnp.concatenate([err_main, err_aux], axis=0)
    full = exchange(jnp.broadcast_to(full[None], (n_lat,) + full.shape), plane)
    sel_all = grow(sel[None], 4)

    both = full.reshape(n_lat, 2, d).transpose(1, 0, 2).reshape(2 * n_lat, d)
    dval = jnp.concatenate([rows_dot(both, dec_rows), rows_dot(both, dec_other)], axis=1)
    dpre = jnp.where(sel[:, :slots] > 0, dval[:n_lat], 0.0) + jnp.where(
        sel[:, slots:] > 0, dval[n_lat:], 0.0
    )

    cut = jnp.concatenate([err_main, err_aux, resid, resid], axis=0)
    cut = cut.reshape(4, n_dp, cols).transpose(1, 0, 2)
    cut, sel_all = lax.optimization_barrier((cut, sel_all))
    cut = jnp.broadcast_to(cut[:, None], (n_dp, side, 4, cols)).reshape(n_dp * side, 4, cols)
    cut = exchange(cut, wide).reshape(2, 2, 2, side, 4, cols)
    sel_all = grow(sel_all, 2)
    dpre_all = grow(dpre.astype(jnp.bfloat16)[None], 4)
    cut, sel_all, dpre_all = lax.optimization_barrier((cut, sel_all, dpre_all))
    for bit in range(3):
        cut = jnp.where((dp >> bit) & 1 == 1, jnp.flip(cut, 2 - bit), cut)
    cut = cut[..., :3, :].transpose(3, 4, 2, 1, 0, 5).reshape(side, 3 * n_dp, cols)
    part = spread(cut, second).reshape(n_lat, 3, n_dp, cols)
    main, aux, res = (part[:, i].reshape(n_lat * n_dp, cols) for i in range(3))
    sel_all = grow(sel_all, 1).transpose(1, 0, 2).reshape(n_lat * n_dp, 2 * slots)
    dpre_all = jnp.concatenate([dpre_all] + [send(dpre_all, step) for step in (2, 1, 3)], axis=0)
    dpre_all = dpre_all.transpose(1, 0, 2).reshape(n_lat * n_dp, slots)

    def half(other):
        def pick(table, i):
            return table[:, i * slots + other * width : i * slots + (other + 1) * width]

        dec_term = cols_dot(pick(sel_all, 0), main) + cols_dot(pick(sel_all, 1), aux)
        return dec_term, cols_dot(pick(dpre_all, 0), res)

    sent = jnp.stack(half(1)).astype(jnp.bfloat16)
    got = lax.ppermute(sent, "inner", swap)
    kept = lax.optimization_barrier(half(0))
    return tuple((kept[i] + got[i].astype(jnp.float32)).astype(jnp.bfloat16) for i in range(2))


def solution(mesh):
    tokens = P(("dp", "lat", "inner"), None)
    shard = ("lat", "inner")
    in_specs = (tokens,) * 3 + (P("dp", None),) * 4 + (P(shard), P(shard), P(shard, None))
    out_specs = (P(shard, "dp"), P(shard, "dp"))
    n_dp, n_lat, n_in = (mesh.shape[a] for a in ("dp", "lat", "inner"))

    def step(*args):
        return local(n_dp, n_lat, n_in, *args)

    return jax.shard_map(step, mesh=mesh, in_specs=in_specs, out_specs=out_specs, check_vma=False)
```

```python
import math

import jax
import jax.numpy as jnp
from jax import lax
from jax.experimental import pallas as pl
from jax.experimental.pallas import tpu as pltpu
from jax.sharding import PartitionSpec as P

LAT_DEV = 32768
BLOCK = 128
LOW = 64


def sel_kernel(place, top_idx, top_val, aux_idx, aux_val, cores, out, high, low, val, found):
    n_top, rows = top_idx.shape
    n_aux = aux_idx.shape[1]
    slots = out.shape[1] // 2
    width = slots // 2
    side = math.isqrt(rows // 2)
    tables = 2 * slots // LOW
    core = place[0]

    def put(at, col, v):
        to = pl.ds(at, col.shape[1])
        high[:, to] = col >> 6
        low[:, to] = col & (LOW - 1)
        val[:, to] = v

    col = aux_idx[...] - place[1] * slots
    inside = (col >= 0) & (col < slots)
    put(0, jnp.where(inside, slots + ((col + core * width) & (slots - 1)), -1), aux_val[...].astype(jnp.float32))
    block, inside = top_idx[...] >> 7, top_idx[...] & (BLOCK - 1)
    col = jnp.full(top_idx.shape, -1, jnp.int32)
    for m in range(slots // BLOCK):
        other, at = divmod(m, width // BLOCK)
        shard = 2 * place[1] + (core if other == 0 else 1 - core)
        number = cores[other : other + 1, width + at : width + at + 1]
        here = (block == number + shard * (LAT_DEV // BLOCK)) & (number >= 0)
        col = jnp.where(here, m * BLOCK + inside, col)
    put(n_aux, col.T, top_val[...].astype(jnp.float32).T)

    n = n_aux + n_top
    row_high = lax.broadcasted_iota(jnp.int32, (tables, n), 0)
    row_low = lax.broadcasted_iota(jnp.int32, (LOW, n), 0)

    def step(a, carry):
        for b in range(side):
            row = jnp.where(core == 0, 2 * (side * a + b), 2 * (side * b + a) + 1)
            one = pl.ds(row, 1)
            spread = jnp.where(row_high == high[one, :n], val[one, :n], 0.0).astype(jnp.bfloat16)
            hot = jnp.where(row_low == low[one, :n], 1.0, 0.0).astype(jnp.bfloat16)
            table = lax.dot_general(
                spread, hot, (((1,), (1,)), ((), ())), preferred_element_type=jnp.float32
            )
            found[pl.ds(side * a + b, tables, stride=side * side), :] = jnp.concatenate([table, table], axis=1)
        return carry

    lax.fori_loop(0, side, step, 0)
    first = lax.broadcasted_iota(jnp.int32, (1, 128), 1) < LOW
    for k in range(2 * slots // 128):
        even = found[2 * k * side * side : (2 * k + 1) * side * side, :]
        odd = found[(2 * k + 1) * side * side : (2 * k + 2) * side * side, :]
        table = jnp.where(first, even, odd)
        if 128 * k >= slots:
            other, at = divmod(128 * k - slots, width)
            table = table * cores[other : other + 1, at : at + 128].astype(jnp.float32)
        out[:, 128 * k : 128 * (k + 1)] = table.astype(out.dtype)


def make_sel(place, top_idx, top_val, aux_idx, aux_val, cores, slots):
    rows = aux_idx.shape[0]
    entries = aux_idx.shape[1] + 128
    whole = pl.BlockSpec(memory_space=pltpu.VMEM)
    return pl.pallas_call(
        sel_kernel,
        in_specs=[pl.BlockSpec(memory_space=pltpu.SMEM)] + [whole] * 5,
        out_specs=whole,
        out_shape=jax.ShapeDtypeStruct((rows // 2, 2 * slots), jnp.bfloat16),
        scratch_shapes=[
            pltpu.VMEM((rows, entries), jnp.int32),
            pltpu.VMEM((rows, entries), jnp.int32),
            pltpu.VMEM((rows, entries), jnp.float32),
            pltpu.VMEM((rows * slots // LOW, 128), jnp.float32),
        ],
        cost_estimate=pl.CostEstimate(
            flops=rows * entries * slots * 32, bytes_accessed=1 << 20, transcendentals=0
        ),
        name="sel",
    )(place, top_idx.T, top_val.T, aux_idx, aux_val, cores)


def rows_dot(left, right):
    return lax.dot_general(
        left, right, (((1,), (1,)), ((), ())), preferred_element_type=jnp.float32
    )


def cols_dot(left, right):
    return lax.dot_general(
        left, right, (((0,), (0,)), ((), ())), preferred_element_type=jnp.float32
    )


def plane_groups(n_dp, side, n_in):
    def device(z, a, b, c):
        y, x = (a, b) if c == 0 else (b, a)
        return ((z * side + y) * side + x) * n_in + c

    ranks, dps, cores = range(side), range(n_dp), range(n_in)
    plane = [[device(z, a, b, c) for a in ranks for b in ranks] for z in dps for c in cores]
    wide = [[device(z, a, b, c) for z in dps for b in ranks] for a in ranks for c in cores]
    second = [[device(z, a, b, c) for a in ranks] for z in dps for b in ranks for c in cores]
    return plane, wide, second


def local(
    n_dp, n_lat, n_in, err_main, err_aux, resid, top_idx, top_val, aux_idx, aux_val, blocks, dead, dec_rows
):
    width, d = dec_rows.shape
    cols = d // n_dp
    slots = width * n_in
    side = math.isqrt(n_lat)
    dp = lax.axis_index("dp")
    lat = lax.axis_index("lat")
    core = lax.axis_index("inner")
    swap = [(i, (i + 1) % n_in) for i in range(n_in)]
    plane, wide, second = plane_groups(n_dp, side, n_in)

    def send(v, step):
        return lax.ppermute(v, "dp", [(i, i ^ step) for i in range(n_dp)])

    def grow(v, step):
        return jnp.concatenate([v, send(v, step)], axis=0)

    def exchange(v, groups):
        return lax.all_to_all(v, ("dp", "lat", "inner"), 0, 0, axis_index_groups=groups, tiled=True)

    def spread(v, groups):
        return exchange(jnp.broadcast_to(v[None], (side,) + v.shape), groups)

    dec_other = lax.ppermute(dec_rows, "inner", swap)
    small = jnp.concatenate([dead, blocks, jnp.zeros((128 - blocks.shape[0],), jnp.int32)])
    small_other = lax.ppermute(small, "inner", swap)
    cores = jnp.stack([small, small_other])
    place = jnp.stack([core, lat])
    sel = make_sel(place, top_idx, top_val, aux_idx, aux_val, cores, slots)

    full = jnp.concatenate([err_main, err_aux], axis=0)
    full = exchange(jnp.broadcast_to(full[None], (n_lat,) + full.shape), plane)
    sel_all = grow(sel[None], 4)

    both = full.reshape(n_lat, 2, d).transpose(1, 0, 2).reshape(2 * n_lat, d)
    dval = jnp.concatenate([rows_dot(both, dec_rows), rows_dot(both, dec_other)], axis=1)
    dpre = jnp.where(sel[:, :slots] > 0, dval[:n_lat], 0.0) + jnp.where(
        sel[:, slots:] > 0, dval[n_lat:], 0.0
    )

    cut = jnp.concatenate([err_main, err_aux, resid, resid], axis=0)
    cut = cut.reshape(4, n_dp, cols).transpose(1, 0, 2)
    cut, sel_all = lax.optimization_barrier((cut, sel_all))
    cut = jnp.broadcast_to(cut[:, None], (n_dp, side, 4, cols)).reshape(n_dp * side, 4, cols)
    cut = exchange(cut, wide).reshape(2, 2, 2, side, 4, cols)
    sel_all = grow(sel_all, 2)
    dpre_all = grow(dpre.astype(jnp.bfloat16)[None], 4)
    cut, sel_all, dpre_all = lax.optimization_barrier((cut, sel_all, dpre_all))
    for bit in range(3):
        cut = jnp.where((dp >> bit) & 1 == 1, jnp.flip(cut, 2 - bit), cut)
    cut = cut[..., :3, :].transpose(3, 4, 2, 1, 0, 5).reshape(side, 3 * n_dp, cols)
    part = spread(cut, second).reshape(n_lat, 3, n_dp, cols)
    main, aux, res = (part[:, i].reshape(n_lat * n_dp, cols) for i in range(3))
    sel_all = grow(sel_all, 1).transpose(1, 0, 2).reshape(n_lat * n_dp, 2 * slots)
    dpre_all = jnp.concatenate([dpre_all] + [send(dpre_all, step) for step in (2, 1, 3)], axis=0)
    dpre_all = dpre_all.transpose(1, 0, 2).reshape(n_lat * n_dp, slots)

    def half(other):
        def pick(table, i):
            return table[:, i * slots + other * width : i * slots + (other + 1) * width]

        dec_term = cols_dot(pick(sel_all, 0), main) + cols_dot(pick(sel_all, 1), aux)
        return dec_term, cols_dot(pick(dpre_all, 0), res)

    sent = jnp.stack(half(1)).astype(jnp.bfloat16)
    got = lax.ppermute(sent, "inner", swap)
    kept = lax.optimization_barrier(half(0))
    return tuple((kept[i] + got[i].astype(jnp.float32)).astype(jnp.bfloat16) for i in range(2))


def solution(mesh):
    tokens = P(("dp", "lat", "inner"), None)
    shard = ("lat", "inner")
    in_specs = (tokens,) * 3 + (P("dp", None),) * 4 + (P(shard), P(shard), P(shard, None))
    out_specs = (P(shard, "dp"), P(shard, "dp"))
    n_dp, n_lat, n_in = (mesh.shape[a] for a in ("dp", "lat", "inner"))

    def step(*args):
        return local(n_dp, n_lat, n_in, *args)

    return jax.shard_map(step, mesh=mesh, in_specs=in_specs, out_specs=out_specs, check_vma=False)
```

```python
import math

import jax
import jax.numpy as jnp
from jax import lax
from jax.experimental import pallas as pl
from jax.experimental.pallas import tpu as pltpu
from jax.sharding import PartitionSpec as P

LAT_DEV = 32768
BLOCK = 128
LOW = 64


def sel_kernel(place, top_idx, top_val, aux_idx, aux_val, cores, out, high, low, val, found):
    n_top, rows = top_idx.shape
    n_aux = aux_idx.shape[1]
    slots = out.shape[1] // 2
    width = slots // 2
    side = math.isqrt(rows // 2)
    tables = 2 * slots // LOW
    core = place[0]

    def put(at, col, v):
        to = pl.ds(at, col.shape[1])
        high[:, to] = col >> 6
        low[:, to] = col & (LOW - 1)
        val[:, to] = v

    col = aux_idx[...] - place[1] * slots
    inside = (col >= 0) & (col < slots)
    put(0, jnp.where(inside, slots + ((col + core * width) & (slots - 1)), -1), aux_val[...].astype(jnp.float32))
    block, inside = top_idx[...] >> 7, top_idx[...] & (BLOCK - 1)
    col = jnp.full(top_idx.shape, -1, jnp.int32)
    for m in range(slots // BLOCK):
        other, at = divmod(m, width // BLOCK)
        shard = 2 * place[1] + (core if other == 0 else 1 - core)
        number = cores[other : other + 1, width + at : width + at + 1]
        here = (block == number + shard * (LAT_DEV // BLOCK)) & (number >= 0)
        col = jnp.where(here, m * BLOCK + inside, col)
    put(n_aux, col.T, top_val[...].astype(jnp.float32).T)

    n = n_aux + n_top
    row_high = lax.broadcasted_iota(jnp.int32, (tables, n), 0)
    row_low = lax.broadcasted_iota(jnp.int32, (LOW, n), 0)

    def step(a, carry):
        for b in range(side):
            row = jnp.where(core == 0, 2 * (side * a + b), 2 * (side * b + a) + 1)
            one = pl.ds(row, 1)
            spread = jnp.where(row_high == high[one, :n], val[one, :n], 0.0).astype(jnp.bfloat16)
            hot = jnp.where(row_low == low[one, :n], 1.0, 0.0).astype(jnp.bfloat16)
            table = lax.dot_general(
                spread, hot, (((1,), (1,)), ((), ())), preferred_element_type=jnp.float32
            )
            found[pl.ds(side * a + b, tables, stride=side * side), :] = jnp.concatenate([table, table], axis=1)
        return carry

    lax.fori_loop(0, side, step, 0)
    first = lax.broadcasted_iota(jnp.int32, (1, 128), 1) < LOW
    for k in range(2 * slots // 128):
        even = found[2 * k * side * side : (2 * k + 1) * side * side, :]
        odd = found[(2 * k + 1) * side * side : (2 * k + 2) * side * side, :]
        table = jnp.where(first, even, odd)
        if 128 * k >= slots:
            other, at = divmod(128 * k - slots, width)
            table = table * cores[other : other + 1, at : at + 128].astype(jnp.float32)
        out[:, 128 * k : 128 * (k + 1)] = table.astype(out.dtype)


def make_sel(place, top_idx, top_val, aux_idx, aux_val, cores, slots):
    rows = aux_idx.shape[0]
    entries = aux_idx.shape[1] + 128
    whole = pl.BlockSpec(memory_space=pltpu.VMEM)
    return pl.pallas_call(
        sel_kernel,
        in_specs=[pl.BlockSpec(memory_space=pltpu.SMEM)] + [whole] * 5,
        out_specs=whole,
        out_shape=jax.ShapeDtypeStruct((rows // 2, 2 * slots), jnp.bfloat16),
        scratch_shapes=[
            pltpu.VMEM((rows, entries), jnp.int32),
            pltpu.VMEM((rows, entries), jnp.int32),
            pltpu.VMEM((rows, entries), jnp.float32),
            pltpu.VMEM((rows * slots // LOW, 128), jnp.float32),
        ],
        cost_estimate=pl.CostEstimate(
            flops=rows * entries * slots * 32, bytes_accessed=1 << 20, transcendentals=0
        ),
        name="sel",
    )(place, top_idx.T, top_val.T, aux_idx, aux_val, cores)


def rows_dot(left, right):
    return lax.dot_general(
        left, right, (((1,), (1,)), ((), ())), preferred_element_type=jnp.float32
    )


def cols_dot(left, right):
    return lax.dot_general(
        left, right, (((0,), (0,)), ((), ())), preferred_element_type=jnp.float32
    )


def plane_groups(n_dp, side, n_in):
    def device(z, a, b, c):
        y, x = (a, b) if c == 0 else (b, a)
        return ((z * side + y) * side + x) * n_in + c

    ranks, dps, cores = range(side), range(n_dp), range(n_in)
    first = [[device(z, a, b, c) for b in ranks] for z in dps for a in ranks for c in cores]
    wide = [[device(z, a, b, c) for z in dps for b in ranks] for a in ranks for c in cores]
    second = [[device(z, a, b, c) for a in ranks] for z in dps for b in ranks for c in cores]
    return first, wide, second


def local(
    n_dp, n_lat, n_in, err_main, err_aux, resid, top_idx, top_val, aux_idx, aux_val, blocks, dead, dec_rows
):
    width, d = dec_rows.shape
    cols = d // n_dp
    slots = width * n_in
    side = math.isqrt(n_lat)
    dp = lax.axis_index("dp")
    lat = lax.axis_index("lat")
    core = lax.axis_index("inner")
    swap = [(i, (i + 1) % n_in) for i in range(n_in)]
    first, wide, second = plane_groups(n_dp, side, n_in)

    def send(v, step):
        return lax.ppermute(v, "dp", [(i, i ^ step) for i in range(n_dp)])

    def grow(v, step):
        return jnp.concatenate([v, send(v, step)], axis=0)

    def exchange(v, groups):
        return lax.all_to_all(v, ("dp", "lat", "inner"), 0, 0, axis_index_groups=groups, tiled=True)

    def spread(v, groups):
        return exchange(jnp.broadcast_to(v[None], (side,) + v.shape), groups)

    dec_other = lax.ppermute(dec_rows, "inner", swap)
    small = jnp.concatenate([dead, blocks, jnp.zeros((128 - blocks.shape[0],), jnp.int32)])
    small_other = lax.ppermute(small, "inner", swap)
    cores = jnp.stack([small, small_other])
    place = jnp.stack([core, lat])
    sel = make_sel(place, top_idx, top_val, aux_idx, aux_val, cores, slots)

    near = spread(jnp.concatenate([err_main, err_aux], axis=0), first)
    near, sel = lax.optimization_barrier((near, sel))
    full = spread(near, second)
    sel_all = grow(sel[None], 4)

    both = full.reshape(n_lat, 2, d).transpose(1, 0, 2).reshape(2 * n_lat, d)
    dval = jnp.concatenate([rows_dot(both, dec_rows), rows_dot(both, dec_other)], axis=1)
    dpre = jnp.where(sel[:, :slots] > 0, dval[:n_lat], 0.0) + jnp.where(
        sel[:, slots:] > 0, dval[n_lat:], 0.0
    )

    cut = jnp.concatenate([err_main, err_aux, resid, resid], axis=0)
    cut = cut.reshape(4, n_dp, cols).transpose(1, 0, 2)
    cut, sel_all = lax.optimization_barrier((cut, sel_all))
    cut = jnp.broadcast_to(cut[:, None], (n_dp, side, 4, cols)).reshape(n_dp * side, 4, cols)
    cut = exchange(cut, wide).reshape(2, 2, 2, side, 4, cols)
    sel_all = grow(sel_all, 2)
    dpre_all = grow(dpre.astype(jnp.bfloat16)[None], 4)
    cut, sel_all, dpre_all = lax.optimization_barrier((cut, sel_all, dpre_all))
    for bit in range(3):
        cut = jnp.where((dp >> bit) & 1 == 1, jnp.flip(cut, 2 - bit), cut)
    cut = cut[..., :3, :].transpose(3, 4, 2, 1, 0, 5).reshape(side, 3 * n_dp, cols)
    part = spread(cut, second).reshape(n_lat, 3, n_dp, cols)
    main, aux, res = (part[:, i].reshape(n_lat * n_dp, cols) for i in range(3))
    sel_all = grow(sel_all, 1).transpose(1, 0, 2).reshape(n_lat * n_dp, 2 * slots)
    dpre_all = jnp.concatenate([dpre_all] + [send(dpre_all, step) for step in (2, 1, 3)], axis=0)
    dpre_all = dpre_all.transpose(1, 0, 2).reshape(n_lat * n_dp, slots)

    def half(other):
        def pick(table, i):
            return table[:, i * slots + other * width : i * slots + (other + 1) * width]

        dec_term = cols_dot(pick(sel_all, 0), main) + cols_dot(pick(sel_all, 1), aux)
        return dec_term, cols_dot(pick(dpre_all, 0), res)

    sent = jnp.stack(half(1)).astype(jnp.bfloat16)
    got = lax.ppermute(sent, "inner", swap)
    kept = lax.optimization_barrier(half(0))
    return tuple((kept[i] + got[i].astype(jnp.float32)).astype(jnp.bfloat16) for i in range(2))


def solution(mesh):
    tokens = P(("dp", "lat", "inner"), None)
    shard = ("lat", "inner")
    in_specs = (tokens,) * 3 + (P("dp", None),) * 4 + (P(shard), P(shard), P(shard, None))
    out_specs = (P(shard, "dp"), P(shard, "dp"))
    n_dp, n_lat, n_in = (mesh.shape[a] for a in ("dp", "lat", "inner"))

    def step(*args):
        return local(n_dp, n_lat, n_in, *args)

    return jax.shard_map(step, mesh=mesh, in_specs=in_specs, out_specs=out_specs, check_vma=False)
```
